32 devices in a mesh: dp: 8 (over y, x, core), tensor: 4 (over z).
Axes of the slice: x: 2, y: 2, z: 4, core: 2. Of those that a mesh axis runs over, the one named last changes fastest.
Arguments:
- resid: bfloat16 [4096, 4096], P('dp', 'tensor'), may hold values from -32 to 32
- hidden: bfloat16 [4096, 14336], P('dp', 'tensor'), may hold values from -6 to 6
- down_weight: bfloat16 [14336, 4096], P('tensor'), may hold values from -1 to 1
- gain: float32 [4096], replicated, may hold values from 0.1 to 1.9
- domain_ids: int32 [8], replicated, may hold values from 0 to 3
Outputs:
- grad_hidden: bfloat16 [4096, 14336], P('dp', 'tensor')
- grad_resid: bfloat16 [4096, 4096], P('dp', 'tensor')
- grad_down: float32 [14336, 4096], P('tensor', 'dp')
- grad_gain: float32 [4096], P('tensor')
The draws below stay inside these ranges and needn't reach their ends.
All inputs are finite; a program needn't handle non-finite values.
Results may differ from the reference program's by a relative error of at most 0.0034.
Values may be sent and summed in bfloat16 or wider, within the bound.
A program may use at most 192 MiB of HBM per device.

```python
import math
import jax
import jax.numpy as jnp
from jax import lax

D = 4096
FF = 14336
SEQ = 128
PAIRS_DEV = 2
DOMAINS = 4
SHARDS = 8
NPAIRS = 16
TOKENS = 4096


def draw_resid(key, part):
    key = jax.random.fold_in(key, 7)
    base_key, row_key, col_key = jax.random.split(key, 3)
    row_scale = jnp.exp(jax.random.uniform(row_key, (TOKENS, 1), jnp.float32, math.log(0.1), 0.0))
    col_pos = jnp.arange(D, dtype=jnp.float32)[None, :] / D
    col_jitter = jax.random.uniform(col_key, (1, D), jnp.float32, 0.7, 1.4)
    col_scale = 0.5 * jnp.exp(math.log(10.0) * col_pos) * col_jitter
    base = jnp.clip(jax.random.normal(base_key, (TOKENS, D), jnp.float32), -4.0, 4.0)
    return (base * row_scale * col_scale).astype(jnp.bfloat16)


def draw_hidden(key, part):
    key = jax.random.fold_in(key, 11)
    base_key, shift_key = jax.random.split(key, 2)
    base = jnp.clip(jax.random.normal(base_key, (TOKENS, FF), jnp.float32), -4.0, 4.0)
    shift = jax.random.uniform(shift_key, (TOKENS, 1), jnp.float32, -0.15, 0.15)
    return (base + shift).astype(jnp.bfloat16)


def draw_down_weight(key, part):
    key = jax.random.fold_in(key, 13)
    base_key, common_key = jax.random.split(key, 2)
    base = jnp.clip(jax.random.normal(base_key, (FF, D), jnp.float32), -3.0, 3.0)
    common = jnp.clip(jax.random.normal(common_key, (1, D), jnp.float32), -3.0, 3.0)
    return (base / math.sqrt(FF) + common * (16.0 / FF)).astype(jnp.bfloat16)


def with_ends(array, own_key, least, high):
    extent = array.shape
    index_at = [jax.random.randint(jax.random.fold_in(own_key, axis), (), 0, extent[axis]) for axis in range(len(extent))]
    array = array.at[tuple(index_at)].set(least)
    longest = extent.index(max(extent))
    index_at[longest] = (index_at[longest] + 1) % extent[longest]
    return array.at[tuple(index_at)].set(high)


def setup_inputs(seed: int = 0) -> dict:
    arg_keys = jax.random.split(jax.random.key(seed), 6)
    return {
        "resid": draw_resid(jax.random.fold_in(arg_keys[5], 71), 0),
        "hidden": draw_hidden(jax.random.fold_in(arg_keys[5], 71), 0),
        "down_weight": draw_down_weight(jax.random.fold_in(arg_keys[5], 71), 0),
        "gain": jnp.clip(1.0 + 0.18 * jax.random.normal(arg_keys[3], (D,), jnp.float32), 0.1, 1.9),
        "domain_ids": with_ends(jax.random.randint(arg_keys[4], (SHARDS,), 0, DOMAINS), jax.random.fold_in(arg_keys[4], 1), 0, DOMAINS - 1).astype(jnp.int32),
    }


score_scale = 20.0
loss_scale = 8192.0
eps_norm = 1e-05
eps_embed = 1e-06

def pool_tokens(layer, gain):
    inverse = lax.rsqrt(lax.optimization_barrier(jnp.mean(layer * layer, axis=1, keepdims=True)) + eps_norm)
    normed = layer * inverse * gain[None, :]
    return lax.optimization_barrier(jnp.mean(normed.reshape(-1, SEQ, D), axis=1))

def objective(pooled, domain_ids):
    pair_view = pooled.reshape(NPAIRS, 2, D)
    pair_norm = jnp.sqrt(lax.optimization_barrier(jnp.sum(pair_view * pair_view, axis=2, keepdims=True)) + eps_embed)
    unit_vecs = pair_view / pair_norm
    scores = score_scale * jnp.dot(unit_vecs[:, 0], unit_vecs[:, 1].T, precision=lax.Precision.HIGHEST)
    owners = jnp.repeat(domain_ids, PAIRS_DEV)
    same_domain = owners[:, None] == owners[None, :]
    row_totals = lax.optimization_barrier(jnp.sum(jnp.where(same_domain, jnp.exp(scores), 0.0), axis=1))
    row_loss = jnp.log(row_totals) - jnp.diagonal(scores)
    return loss_scale * jnp.sum(row_loss)

def reference(resid, hidden, down_weight, gain, domain_ids):
    layer = resid.astype(jnp.float32) + jnp.dot(hidden, down_weight, preferred_element_type=jnp.float32)
    pooled, pull_back = jax.vjp(pool_tokens, layer, gain)
    d_pooled = jax.grad(objective)(pooled, domain_ids)
    d_layer, grad_gain = pull_back(d_pooled)
    grad_resid = d_layer.astype(jnp.bfloat16)
    grad_hidden = jnp.dot(grad_resid, down_weight.T, preferred_element_type=jnp.float32).astype(jnp.bfloat16)
    hidden_blocks = hidden.reshape(SHARDS, -1, FF)
    grad_blocks = grad_resid.reshape(SHARDS, -1, D)

    def add_shard(running, operands):
        hidden_blk, grad_blk = operands
        partial_sum = jnp.dot(hidden_blk.T, grad_blk, preferred_element_type=jnp.float32)
        return (running + partial_sum, None)
    grad_down, _ = lax.scan(add_shard, jnp.zeros((FF, D), jnp.float32), (hidden_blocks, grad_blocks))
    return (grad_hidden, grad_resid, grad_down, grad_gain)
```

```python
import jax
import jax.numpy as jnp
from jax import lax
from jax.sharding import PartitionSpec as P

SEQ = 128


score_scale = 20.0
loss_scale = 8192.0
eps_norm = 1e-05
eps_embed = 1e-06
highest = lax.Precision.HIGHEST


def shift_perm(size, step):
    return [(i, (i + step) % size) for i in range(size)]


def flip_perm(size, mask):
    return [(i, i ^ mask) for i in range(size)]


def score_gradient(scores, allowed, target):
    weights = jnp.where(allowed, jnp.exp(scores), 0.0)
    soft_weights = weights / jnp.sum(weights, axis=1, keepdims=True)
    return loss_scale * (soft_weights - target.astype(jnp.float32))


def summed_slab(resid, hidden, down_weight, slab_width, rank, ranks):
    received = []
    for step in list(range(ranks // 2, 0, -1)) + list(range(ranks // 2 + 1, ranks)):
        target = lax.rem(rank + step, ranks)
        block = lax.dynamic_slice_in_dim(down_weight, target * slab_width, slab_width, 1)
        part = jnp.dot(hidden, block, preferred_element_type=jnp.float32)
        row_top = jnp.maximum(jnp.max(jnp.abs(part), axis=1, keepdims=True), 1e-30)
        low = (part / row_top).astype(jnp.float16)
        perm = shift_perm(ranks, step)
        received.append((lax.ppermute(low, "tensor", perm), lax.ppermute(row_top, "tensor", perm)))
    block = lax.dynamic_slice_in_dim(down_weight, rank * slab_width, slab_width, 1)
    layer = jnp.dot(hidden, block, preferred_element_type=jnp.float32) + resid.astype(jnp.float32)
    for low, row_top in received:
        layer = layer + low.astype(jnp.float32) * row_top
    return layer


def gathered_columns(slab, rank, ranks):
    width = slab.shape[1]
    whole = jnp.zeros((slab.shape[0], width * ranks), slab.dtype)
    whole = lax.dynamic_update_slice_in_dim(whole, slab, rank * width, 1)
    for step in range(1, ranks):
        piece = lax.ppermute(slab, "tensor", shift_perm(ranks, step))
        whole = lax.dynamic_update_slice_in_dim(
            whole, piece, lax.rem(rank + ranks - step, ranks) * width, 1
        )
    return whole


def exchanged_tokens(whole, index, count):
    width = whole.shape[1] // count
    blocks = []
    for mask in range(count):
        block = lax.dynamic_slice_in_dim(whole, (index ^ mask) * width, width, 1)
        blocks.append(lax.ppermute(block, "dp", flip_perm(count, mask)) if mask else block)
    return jnp.concatenate(blocks, axis=0)


def gathered_tokens(hidden, count):
    bits = [1 << b for b in range(1, count.bit_length() - 1)]
    rows = hidden.shape[0] // 2
    halves = []
    for part, order in ((hidden[:rows], bits), (hidden[rows:], bits[::-1])):
        pieces = {0: part}
        for bit in order + [1]:
            for mask, piece in list(pieces.items()):
                pieces[mask ^ bit] = lax.ppermute(piece, "dp", flip_perm(count, bit))
        halves.append(pieces)
    return jnp.concatenate([half[mask] for mask in range(count) for half in halves], axis=0)


def pooled_gradient(pooled, domain_ids, pairs_here):
    pairs = pooled.reshape(-1, 2, pooled.shape[1])
    queries = pairs[:, 0]
    passages = pairs[:, 1]
    total_pairs = queries.shape[0]
    owners = jnp.repeat(domain_ids, pairs_here)
    query_norm = jnp.sqrt(jnp.sum(queries * queries, axis=1) + eps_embed)
    passage_norm = jnp.sqrt(jnp.sum(passages * passages, axis=1) + eps_embed)
    query_unit = queries / query_norm[:, None]
    passage_unit = passages / passage_norm[:, None]
    scores = score_scale * jnp.dot(query_unit, passage_unit.T, precision=highest)
    allowed = owners[:, None] == owners[None, :]
    d_score = score_gradient(scores, allowed, jnp.eye(total_pairs))
    weighted = d_score * scores
    d_query = (
        score_scale * jnp.dot(d_score, passage_unit, precision=highest)
        - query_unit * jnp.sum(weighted, axis=1)[:, None]
    ) / query_norm[:, None]
    d_passage = (
        score_scale * jnp.dot(d_score.T, query_unit, precision=highest)
        - passage_unit * jnp.sum(weighted, axis=0)[:, None]
    ) / passage_norm[:, None]
    return jnp.stack((d_query, d_passage), axis=1).reshape(pooled.shape)


def per_device(resid, hidden, down_weight, gain, domain_ids):
    tok_rows = hidden.shape[0]
    model_width = down_weight.shape[1]
    ranks = lax.axis_size("tensor")
    shards = lax.axis_size("dp")
    slab_width = model_width // ranks
    col_width = model_width // shards
    rank = lax.axis_index("tensor")
    shard = lax.axis_index("dp")
    seqs_here = tok_rows // SEQ
    pairs_here = seqs_here // 2

    hidden_all = gathered_tokens(hidden, shards)
    layer = summed_slab(resid, hidden, down_weight, slab_width, rank, ranks)
    layer_low = layer.astype(jnp.bfloat16)
    whole_low = gathered_columns(layer_low, rank, ranks)
    token_cols = exchanged_tokens(whole_low, shard, shards)

    squares = lax.psum(jnp.sum(layer * layer, axis=1), "tensor")
    inverse = lax.rsqrt(squares / model_width + eps_norm)
    raw = jnp.mean((layer * inverse[:, None]).reshape(seqs_here, SEQ, -1), axis=1)
    raw_all = lax.all_gather(raw, ("dp", "tensor"), axis=0, tiled=False)
    raw_all = raw_all.reshape(shards, ranks, seqs_here, slab_width)
    raw_all = jnp.swapaxes(raw_all, 1, 2).reshape(shards * seqs_here, model_width)
    d_pooled = pooled_gradient(raw_all * gain[None, :], domain_ids, pairs_here)
    gain_terms = jnp.sum(d_pooled * raw_all, axis=0)
    grad_gain = lax.dynamic_slice_in_dim(gain_terms, rank * slab_width, slab_width, 0)

    scaled = d_pooled * (gain / SEQ)[None, :]
    scaled_own = lax.dynamic_slice_in_dim(scaled, shard * seqs_here, seqs_here, 0)
    whole_view = whole_low.astype(jnp.float32).reshape(seqs_here, SEQ, model_width)
    along = jnp.sum(scaled_own[:, None, :] * whole_view, axis=2).reshape(tok_rows)
    pull = inverse * inverse * inverse * along / model_width
    own_rows = (
        inverse.reshape(seqs_here, SEQ, 1) * scaled_own[:, None, :]
        - whole_view * pull.reshape(seqs_here, SEQ, 1)
    )
    d_low = own_rows.astype(jnp.bfloat16).reshape(tok_rows, model_width)
    hidden_grad32 = lax.dot_general(
        d_low, down_weight, (((1,), (1,)), ((), ())), preferred_element_type=jnp.float32
    )
    scaled_slab = lax.dynamic_slice_in_dim(scaled_own, rank * slab_width, slab_width, 1)
    grad_resid = (
        inverse.reshape(seqs_here, SEQ, 1) * scaled_slab[:, None, :]
        - layer.reshape(seqs_here, SEQ, slab_width) * pull.reshape(seqs_here, SEQ, 1)
    ).astype(jnp.bfloat16).reshape(tok_rows, slab_width)

    order = shard ^ jnp.arange(shards)
    factors = lax.all_gather(jnp.stack((inverse, pull)), "dp", axis=0, tiled=False)[order]
    inverse_all = factors[:, 0].reshape(shards * seqs_here, SEQ, 1)
    pull_all = factors[:, 1].reshape(shards * seqs_here, SEQ, 1)
    scaled_cols = lax.dynamic_slice_in_dim(scaled, shard * col_width, col_width, 1)
    scaled_cols = scaled_cols.reshape(shards, seqs_here, col_width)[order]
    scaled_cols = scaled_cols.reshape(shards * seqs_here, col_width)
    cols_view = token_cols.astype(jnp.float32).reshape(shards * seqs_here, SEQ, col_width)
    d_cols = (inverse_all * scaled_cols[:, None, :] - cols_view * pull_all).astype(jnp.bfloat16)
    grad_down = lax.dot_general(
        hidden_all,
        d_cols.reshape(shards * tok_rows, col_width),
        (((0,), (0,)), ((), ())),
        preferred_element_type=jnp.float32,
    )
    return (hidden_grad32.astype(jnp.bfloat16), grad_resid, grad_down, grad_gain)


def solution(mesh):
    return jax.shard_map(
        per_device,
        mesh=mesh,
        in_specs=(P("dp", "tensor"), P("dp", "tensor"), P("tensor", None), P(), P()),
        out_specs=(P("dp", "tensor"), P("dp", "tensor"), P("tensor", "dp"), P("tensor")),
        check_vma=False,
    )
```

```python
import jax
import jax.numpy as jnp
from jax import lax
from jax.sharding import PartitionSpec as P

SEQ = 128


score_scale = 20.0
loss_scale = 8192.0
eps_norm = 1e-05
eps_embed = 1e-06
highest = lax.Precision.HIGHEST


def shift_perm(size, step):
    return [(i, (i + step) % size) for i in range(size)]


def flip_perm(size, mask):
    return [(i, i ^ mask) for i in range(size)]


def score_gradient(scores, allowed, target):
    weights = jnp.where(allowed, jnp.exp(scores), 0.0)
    soft_weights = weights / jnp.sum(weights, axis=1, keepdims=True)
    return loss_scale * (soft_weights - target.astype(jnp.float32))


def summed_slab(resid, hidden, down_weight, slab_width, rank, ranks):
    received = []
    for step in list(range(ranks // 2, 0, -1)) + list(range(ranks // 2 + 1, ranks)):
        target = lax.rem(rank + step, ranks)
        block = lax.dynamic_slice_in_dim(down_weight, target * slab_width, slab_width, 1)
        part = jnp.dot(hidden, block, preferred_element_type=jnp.float32)
        row_top = jnp.maximum(jnp.max(jnp.abs(part), axis=1, keepdims=True), 1e-30)
        low = (part / row_top).astype(jnp.float16)
        perm = shift_perm(ranks, step)
        received.append((lax.ppermute(low, "tensor", perm), lax.ppermute(row_top, "tensor", perm)))
    block = lax.dynamic_slice_in_dim(down_weight, rank * slab_width, slab_width, 1)
    layer = jnp.dot(hidden, block, preferred_element_type=jnp.float32) + resid.astype(jnp.float32)
    for low, row_top in received:
        layer = layer + low.astype(jnp.float32) * row_top
    return layer


def gathered_columns(slab, rank, ranks):
    width = slab.shape[1]
    whole = jnp.zeros((slab.shape[0], width * ranks), slab.dtype)
    whole = lax.dynamic_update_slice_in_dim(whole, slab, rank * width, 1)
    for step in range(1, ranks):
        piece = lax.ppermute(slab, "tensor", shift_perm(ranks, step))
        whole = lax.dynamic_update_slice_in_dim(
            whole, piece, lax.rem(rank + ranks - step, ranks) * width, 1
        )
    return whole


def exchanged_tokens(whole, index, count):
    rows = whole.shape[0]
    width = whole.shape[1] // count
    tokens = jnp.zeros((count, rows, width), whole.dtype)
    for mask in range(count):
        other = index ^ mask
        block = lax.dynamic_slice_in_dim(whole, other * width, width, 1)
        if mask:
            block = lax.ppermute(block, "dp", flip_perm(count, mask))
        tokens = lax.dynamic_update_slice_in_dim(tokens, block[None], other, 0)
    return tokens


def pooled_gradient(pooled, domain_ids, pairs_here):
    pairs = pooled.reshape(-1, 2, pooled.shape[1])
    queries = pairs[:, 0]
    passages = pairs[:, 1]
    total_pairs = queries.shape[0]
    owners = jnp.repeat(domain_ids, pairs_here)
    query_norm = jnp.sqrt(jnp.sum(queries * queries, axis=1) + eps_embed)
    passage_norm = jnp.sqrt(jnp.sum(passages * passages, axis=1) + eps_embed)
    query_unit = queries / query_norm[:, None]
    passage_unit = passages / passage_norm[:, None]
    scores = score_scale * jnp.dot(query_unit, passage_unit.T, precision=highest)
    allowed = owners[:, None] == owners[None, :]
    d_score = score_gradient(scores, allowed, jnp.eye(total_pairs))
    weighted = d_score * scores
    d_query = (
        score_scale * jnp.dot(d_score, passage_unit, precision=highest)
        - query_unit * jnp.sum(weighted, axis=1)[:, None]
    ) / query_norm[:, None]
    d_passage = (
        score_scale * jnp.dot(d_score.T, query_unit, precision=highest)
        - passage_unit * jnp.sum(weighted, axis=0)[:, None]
    ) / passage_norm[:, None]
    return jnp.stack((d_query, d_passage), axis=1).reshape(pooled.shape)


def per_device(resid, hidden, down_weight, gain, domain_ids):
    tok_rows = hidden.shape[0]
    model_width = down_weight.shape[1]
    ranks = lax.axis_size("tensor")
    shards = lax.axis_size("dp")
    slab_width = model_width // ranks
    col_width = model_width // shards
    rank = lax.axis_index("tensor")
    shard = lax.axis_index("dp")
    seqs_here = tok_rows // SEQ
    pairs_here = seqs_here // 2

    hidden_all = lax.all_gather(hidden, "dp", axis=0, tiled=True)
    layer = summed_slab(resid, hidden, down_weight, slab_width, rank, ranks)
    squares = lax.psum(jnp.sum(layer * layer, axis=1), "tensor")
    squares, layer_low = lax.optimization_barrier((squares, layer.astype(jnp.bfloat16)))
    whole_low = gathered_columns(layer_low, rank, ranks)
    token_cols = exchanged_tokens(whole_low, shard, shards)
    inverse = lax.rsqrt(squares / model_width + eps_norm)
    raw = jnp.mean((layer * inverse[:, None]).reshape(seqs_here, SEQ, -1), axis=1)
    raw_all = lax.all_gather(raw, ("dp", "tensor"), axis=0, tiled=False)
    raw_all = raw_all.reshape(shards, ranks, seqs_here, slab_width)
    raw_all = jnp.swapaxes(raw_all, 1, 2).reshape(shards * seqs_here, model_width)
    d_pooled = pooled_gradient(raw_all * gain[None, :], domain_ids, pairs_here)
    gain_terms = jnp.sum(d_pooled * raw_all, axis=0)
    grad_gain = lax.dynamic_slice_in_dim(gain_terms, rank * slab_width, slab_width, 0)

    scaled = d_pooled * (gain / SEQ)[None, :]
    scaled_own = lax.dynamic_slice_in_dim(scaled, shard * seqs_here, seqs_here, 0)
    whole_view = whole_low.astype(jnp.float32).reshape(seqs_here, SEQ, model_width)
    along = jnp.sum(scaled_own[:, None, :] * whole_view, axis=2).reshape(tok_rows)
    pull = inverse * inverse * inverse * along / model_width
    own_rows = (
        inverse.reshape(seqs_here, SEQ, 1) * scaled_own[:, None, :]
        - whole_view * pull.reshape(seqs_here, SEQ, 1)
    )
    d_low = own_rows.astype(jnp.bfloat16).reshape(tok_rows, model_width)
    hidden_grad32 = lax.dot_general(
        d_low, down_weight, (((1,), (1,)), ((), ())), preferred_element_type=jnp.float32
    )
    scaled_slab = lax.dynamic_slice_in_dim(scaled_own, rank * slab_width, slab_width, 1)
    grad_resid = (
        inverse.reshape(seqs_here, SEQ, 1) * scaled_slab[:, None, :]
        - layer.reshape(seqs_here, SEQ, slab_width) * pull.reshape(seqs_here, SEQ, 1)
    ).astype(jnp.bfloat16).reshape(tok_rows, slab_width)

    factors = lax.all_gather(jnp.stack((inverse, pull)), "dp", axis=0, tiled=False)
    inverse_all = factors[:, 0].reshape(shards * seqs_here, SEQ, 1)
    pull_all = factors[:, 1].reshape(shards * seqs_here, SEQ, 1)
    scaled_cols = lax.dynamic_slice_in_dim(scaled, shard * col_width, col_width, 1)
    cols_view = token_cols.astype(jnp.float32).reshape(shards * seqs_here, SEQ, col_width)
    d_cols = (inverse_all * scaled_cols[:, None, :] - cols_view * pull_all).astype(jnp.bfloat16)
    grad_down = lax.dot_general(
        hidden_all,
        d_cols.reshape(shards * tok_rows, col_width),
        (((0,), (0,)), ((), ())),
        preferred_element_type=jnp.float32,
    )
    return (hidden_grad32.astype(jnp.bfloat16), grad_resid, grad_down, grad_gain)


def solution(mesh):
    return jax.shard_map(
        per_device,
        mesh=mesh,
        in_specs=(P("dp", "tensor"), P("dp", "tensor"), P("tensor", None), P(), P()),
        out_specs=(P("dp", "tensor"), P("dp", "tensor"), P("tensor", "dp"), P("tensor")),
        check_vma=False,
    )
```

```python
import jax
import jax.numpy as jnp
from jax import lax
from jax.sharding import PartitionSpec as P

SEQ = 128


score_scale = 20.0
loss_scale = 8192.0
eps_norm = 1e-05
eps_embed = 1e-06
highest = lax.Precision.HIGHEST


def shift_perm(size, step):
    return [(i, (i + step) % size) for i in range(size)]


def flip_perm(size, mask):
    return [(i, i ^ mask) for i in range(size)]


def score_gradient(scores, allowed, target):
    weights = jnp.where(allowed, jnp.exp(scores), 0.0)
    soft_weights = weights / jnp.sum(weights, axis=1, keepdims=True)
    return loss_scale * (soft_weights - target.astype(jnp.float32))


def summed_slab(resid, hidden, down_weight, slab_width, rank, ranks):
    received = []
    for step in list(range(ranks // 2, 0, -1)) + list(range(ranks // 2 + 1, ranks)):
        target = lax.rem(rank + step, ranks)
        block = lax.dynamic_slice_in_dim(down_weight, target * slab_width, slab_width, 1)
        part = jnp.dot(hidden, block, preferred_element_type=jnp.float32)
        row_top = jnp.maximum(jnp.max(jnp.abs(part), axis=1, keepdims=True), 1e-30)
        low = (part / row_top).astype(jnp.float16)
        perm = shift_perm(ranks, step)
        received.append((lax.ppermute(low, "tensor", perm), lax.ppermute(row_top, "tensor", perm)))
    block = lax.dynamic_slice_in_dim(down_weight, rank * slab_width, slab_width, 1)
    layer = jnp.dot(hidden, block, preferred_element_type=jnp.float32) + resid.astype(jnp.float32)
    for low, row_top in received:
        layer = layer + low.astype(jnp.float32) * row_top
    return layer


def gathered_columns(slab, rank, ranks):
    width = slab.shape[1]
    whole = jnp.zeros((slab.shape[0], width * ranks), slab.dtype)
    whole = lax.dynamic_update_slice_in_dim(whole, slab, rank * width, 1)
    for step in range(1, ranks):
        piece = lax.ppermute(slab, "tensor", shift_perm(ranks, step))
        whole = lax.dynamic_update_slice_in_dim(
            whole, piece, lax.rem(rank + ranks - step, ranks) * width, 1
        )
    return whole


def exchanged_tokens(whole, index, count):
    rows = whole.shape[0]
    width = whole.shape[1] // count
    tokens = jnp.zeros((count, rows, width), whole.dtype)
    for mask in range(count):
        other = index ^ mask
        block = lax.dynamic_slice_in_dim(whole, other * width, width, 1)
        if mask:
            block = lax.ppermute(block, "dp", flip_perm(count, mask))
        tokens = lax.dynamic_update_slice_in_dim(tokens, block[None], other, 0)
    return tokens


def pooled_gradient(pooled, domain_ids, pairs_here):
    pairs = pooled.reshape(-1, 2, pooled.shape[1])
    queries = pairs[:, 0]
    passages = pairs[:, 1]
    total_pairs = queries.shape[0]
    owners = jnp.repeat(domain_ids, pairs_here)
    query_norm = jnp.sqrt(jnp.sum(queries * queries, axis=1) + eps_embed)
    passage_norm = jnp.sqrt(jnp.sum(passages * passages, axis=1) + eps_embed)
    query_unit = queries / query_norm[:, None]
    passage_unit = passages / passage_norm[:, None]
    scores = score_scale * jnp.dot(query_unit, passage_unit.T, precision=highest)
    allowed = owners[:, None] == owners[None, :]
    d_score = score_gradient(scores, allowed, jnp.eye(total_pairs))
    weighted = d_score * scores
    d_query = (
        score_scale * jnp.dot(d_score, passage_unit, precision=highest)
        - query_unit * jnp.sum(weighted, axis=1)[:, None]
    ) / query_norm[:, None]
    d_passage = (
        score_scale * jnp.dot(d_score.T, query_unit, precision=highest)
        - passage_unit * jnp.sum(weighted, axis=0)[:, None]
    ) / passage_norm[:, None]
    return jnp.stack((d_query, d_passage), axis=1).reshape(pooled.shape)


def per_device(resid, hidden, down_weight, gain, domain_ids):
    tok_rows = hidden.shape[0]
    model_width = down_weight.shape[1]
    ranks = lax.axis_size("tensor")
    shards = lax.axis_size("dp")
    slab_width = model_width // ranks
    col_width = model_width // shards
    rank = lax.axis_index("tensor")
    shard = lax.axis_index("dp")
    seqs_here = tok_rows // SEQ
    pairs_here = seqs_here // 2

    hidden_all = lax.all_gather(hidden, "dp", axis=0, tiled=True)
    layer = summed_slab(resid, hidden, down_weight, slab_width, rank, ranks)
    squares = lax.psum(jnp.sum(layer * layer, axis=1), "tensor")
    inverse = lax.rsqrt(squares / model_width + eps_norm)
    raw = jnp.mean((layer * inverse[:, None]).reshape(seqs_here, SEQ, -1), axis=1)
    raw = lax.all_gather(raw, "tensor", axis=1, tiled=True)
    raw, layer_low = lax.optimization_barrier((raw, layer.astype(jnp.bfloat16)))
    whole_low = gathered_columns(layer_low, rank, ranks)
    raw_all = lax.all_gather(raw, "dp", axis=0, tiled=True)
    d_pooled = pooled_gradient(raw_all * gain[None, :], domain_ids, pairs_here)
    gain_terms = jnp.sum(d_pooled * raw_all, axis=0)
    grad_gain = lax.dynamic_slice_in_dim(gain_terms, rank * slab_width, slab_width, 0)

    scaled = d_pooled * (gain / SEQ)[None, :]
    scaled_own = lax.dynamic_slice_in_dim(scaled, shard * seqs_here, seqs_here, 0)
    whole_view = whole_low.astype(jnp.float32).reshape(seqs_here, SEQ, model_width)
    along = jnp.sum(scaled_own[:, None, :] * whole_view, axis=2).reshape(tok_rows)
    pull = inverse * inverse * inverse * along / model_width
    own_rows = (
        inverse.reshape(seqs_here, SEQ, 1) * scaled_own[:, None, :]
        - whole_view * pull.reshape(seqs_here, SEQ, 1)
    )
    d_low = own_rows.astype(jnp.bfloat16).reshape(tok_rows, model_width)
    hidden_grad32 = lax.dot_general(
        d_low, down_weight, (((1,), (1,)), ((), ())), preferred_element_type=jnp.float32
    )
    scaled_slab = lax.dynamic_slice_in_dim(scaled_own, rank * slab_width, slab_width, 1)
    grad_resid = (
        inverse.reshape(seqs_here, SEQ, 1) * scaled_slab[:, None, :]
        - layer.reshape(seqs_here, SEQ, slab_width) * pull.reshape(seqs_here, SEQ, 1)
    ).astype(jnp.bfloat16).reshape(tok_rows, slab_width)

    factors = lax.all_gather(jnp.stack((inverse, pull)), "dp", axis=0, tiled=False)
    factors, whole_low = lax.optimization_barrier((factors, whole_low))
    token_cols = exchanged_tokens(whole_low, shard, shards)
    inverse_all = factors[:, 0].reshape(shards * seqs_here, SEQ, 1)
    pull_all = factors[:, 1].reshape(shards * seqs_here, SEQ, 1)
    scaled_cols = lax.dynamic_slice_in_dim(scaled, shard * col_width, col_width, 1)
    cols_view = token_cols.astype(jnp.float32).reshape(shards * seqs_here, SEQ, col_width)
    d_cols = (inverse_all * scaled_cols[:, None, :] - cols_view * pull_all).astype(jnp.bfloat16)
    grad_down = lax.dot_general(
        hidden_all,
        d_cols.reshape(shards * tok_rows, col_width),
        (((0,), (0,)), ((), ())),
        preferred_element_type=jnp.float32,
    )
    return (hidden_grad32.astype(jnp.bfloat16), grad_resid, grad_down, grad_gain)


def solution(mesh):
    return jax.shard_map(
        per_device,
        mesh=mesh,
        in_specs=(P("dp", "tensor"), P("dp", "tensor"), P("tensor", None), P(), P()),
        out_specs=(P("dp", "tensor"), P("dp", "tensor"), P("tensor", "dp"), P("tensor")),
        check_vma=False,
    )
```
